32 devices in a mesh: dp: 8 (over z, x), expert: 4 (over y, core).
Axes of the slice: x: 2, y: 2, z: 4, core: 2. Of those that a mesh axis runs over, the one named last changes fastest.
Arguments:
- x_act: bfloat16 [8, 4, 256, 4096], P('dp', None, None, 'expert'), may hold values from -16 to 16
- d_out: bfloat16 [8, 4, 256, 1536], P('dp'), may hold values from -0.375 to 0.375
- error: bfloat16 [8, 4, 4096, 1536], P('dp', None, 'expert'), may hold values from -6 to 6
- q_init: bfloat16 [1536, 256], replicated, may hold values from -6 to 6
- modality: int32 [4], replicated, may hold values from 0 to 1, as said below
- membership: int32 [8], replicated, may hold values from 0 to 3, as said below
Outputs:
- q_sum: bfloat16 [8, 1536, 256], P('dp')
- error_new: bfloat16 [8, 4, 4096, 1536], P('dp', None, 'expert')
The draws below stay inside these ranges and needn't reach their ends.
Inputs may be any that keep to these rules, and one draw needn't show every extreme that they name: Half of the experts have modality 0 and half modality 1. `membership`: each text replica group holds exactly 2 data replicas.
All inputs are finite; a program needn't handle non-finite values.
Results may differ from the reference program's by a relative error of at most 0.005.
Values may be sent and summed in bfloat16 or wider, within the bound.
A program may use at most 128 MiB of HBM per device.

```python
import jax
import jax.numpy as jnp
from jax import lax

D = 4096
H = 1536
R = 64
GROUPS = 4
EXPERTS = 4
TOK = 256
REPL = 2
N_DP = 8


def draw_modality(key, part):
    return (jax.random.permutation(key, EXPERTS) % 2).astype(jnp.int32)


def draw_membership(key, part):
    return (jax.random.permutation(key, GROUPS * REPL) // REPL).astype(jnp.int32)


def draw_x_act(key, part):
    key_rough, key_noise = jax.random.split(jax.random.fold_in(key, 17), 2)
    replicas = GROUPS * REPL
    feature = jnp.arange(D, dtype=jnp.float32) / D
    tilt = jnp.exp(jnp.log(3.0) * (feature - 0.5))
    rough = jnp.exp(jax.random.uniform(key_rough, (replicas, EXPERTS, 1, D), minval=-1.15, maxval=1.15))
    noise = jnp.clip(jax.random.normal(key_noise, (replicas, EXPERTS, TOK, D)), -4.0, 4.0)
    return jnp.clip(noise * rough * tilt, -16.0, 16.0).astype(jnp.bfloat16)


def steps_of(rng, shape, cuts, least, high):
    loudness, own = 1.0, jax.random.fold_in(rng, 6)
    for axis_at, parts in cuts:
        draws = jnp.exp(jax.random.uniform(jax.random.fold_in(own, axis_at), (parts,), jnp.float32, least / len(cuts), high / len(cuts)))
        loudness = loudness * jnp.repeat(draws, shape[axis_at] // parts).reshape([-1 if axis == axis_at else 1 for axis in range(len(shape))])
    return loudness


def gaussian(stream_key, extent, spread, most, shards=(), held_as=jnp.bfloat16):
    level = steps_of(stream_key, extent, shards, -0.22, 0.18) if shards else 1.0
    entries = jax.random.normal(stream_key, extent, jnp.float32) * spread * level
    return jnp.minimum(jnp.maximum(entries, -most), most).astype(held_as)


def setup_inputs(seed: int = 0) -> dict:
    splits = jax.random.split(jax.random.key(seed), 7)
    x_act = draw_x_act(jax.random.fold_in(splits[6], 71), 0)
    d_out = gaussian(splits[1], (N_DP, EXPERTS, TOK, H), (TOK ** -0.5), 0.375, ((0, 8),))
    error = gaussian(splits[2], (N_DP, EXPERTS, D, H), 1.0, 6.0, ((0, 8), (2, 4)))
    q_init = gaussian(splits[3], (H, EXPERTS * R), 1.0, 6.0)
    modality = draw_modality(jax.random.fold_in(splits[6], 71), 0)
    membership = draw_membership(jax.random.fold_in(splits[6], 71), 0)
    return {"x_act": x_act, "d_out": d_out, "error": error, "q_init": q_init, "modality": modality, "membership": membership}


highest = lax.Precision.HIGHEST

def average(values, modality, membership):
    replicas = membership.shape[0]
    same_group = (membership[:, None] == membership[None, :]).astype(jnp.float32) / REPL
    group_mean = jnp.einsum('ij,jabc->iabc', same_group, values, precision=highest)
    whole_mean = jnp.broadcast_to(jnp.sum(values, axis=0, keepdims=True) / replicas, values.shape)
    image_blocks = (modality == 0)[:, None]
    return jnp.where(image_blocks, whole_mean, group_mean)

def reference(x_act, d_out, error, q_init, modality, membership):
    q_blocks = q_init.reshape(H, EXPERTS, R).astype(jnp.float32)

    def left_of(inputs):
        tok_x, grads_out, residual = inputs
        gradient = jnp.einsum('ktd,kth->kdh', tok_x.astype(jnp.float32), grads_out.astype(jnp.float32), precision=highest)
        merged = (gradient + residual.astype(jnp.float32)).astype(jnp.bfloat16)
        left_part = jnp.einsum('kdh,hkr->dkr', merged.astype(jnp.float32), q_blocks, precision=highest)
        return (merged, left_part)
    merged, left_part = lax.map(left_of, (x_act, d_out, error))
    left_mean = average(left_part, modality, membership)
    gram_block = jnp.einsum('idkr,idks->ikrs', left_mean, left_mean, precision=highest)
    identity = jnp.eye(R, dtype=jnp.float32)
    shift_term = 0.001 * jnp.trace(gram_block, axis1=2, axis2=3) / R
    factor_low = jnp.linalg.cholesky(gram_block + shift_term[:, :, None, None] * identity)
    inverse = jax.scipy.linalg.solve_triangular(factor_low, jnp.broadcast_to(identity, factor_low.shape), lower=True)
    p_hat = jnp.einsum('idkr,iksr->idks', left_mean, inverse, precision=highest).astype(jnp.bfloat16)

    def right_of(inputs):
        merged_one, p_one = inputs
        return jnp.einsum('kdh,dkr->hkr', merged_one.astype(jnp.float32), p_one.astype(jnp.float32), precision=highest)
    q_local = lax.map(right_of, (merged, p_hat))
    q_sum = average(q_local, modality, membership).astype(jnp.bfloat16)

    def error_of(inputs):
        merged_one, p_one, q_one = inputs
        approx = jnp.einsum('dkr,hkr->kdh', p_one.astype(jnp.float32), q_one.astype(jnp.float32), precision=highest)
        return (merged_one.astype(jnp.float32) - approx).astype(jnp.bfloat16)
    error_new = lax.map(error_of, (merged, p_hat, q_sum))
    replicas = membership.shape[0]
    return (q_sum.reshape(replicas, H, EXPERTS * R), error_new)
```

```python
import functools

import jax
import jax.numpy as jnp
from jax import lax
from jax.experimental import pallas as pl
from jax.experimental.pallas import tpu as pltpu
from jax.sharding import PartitionSpec as P

GROUPS = 4


highest = lax.Precision.HIGHEST


def split_columns(values, order, rank_width, group_mask):
    count = values.shape[0]
    experts_here = order.shape[0]
    half = experts_here // 2
    taken = jnp.take(values.reshape(count, experts_here, rank_width), order, axis=1)
    image_part = taken[:, :half].reshape(count, half * rank_width)
    text_part = taken[:, half:].reshape(count, half * rank_width)
    return (image_part, group_mask[:, None, None] * text_part)


def join_columns(image_sum, text_slots, rank_of, group_mask, rank_width, replicas, group_size):
    count = image_sum.shape[0]
    half = image_sum.shape[1] // rank_width
    image_mean = (image_sum / replicas).reshape(count, half, rank_width)
    text_mean = (jnp.sum(group_mask[:, None, None] * text_slots, axis=0) / group_size).reshape(
        count, half, rank_width
    )
    joined = jnp.concatenate([image_mean, text_mean], axis=1)
    return jnp.take(joined, rank_of, axis=1).reshape(count, 2 * half * rank_width)


def on_device(x_act, d_out, error, q_init, modality, membership):
    tok_x = x_act[0]
    grads_out = d_out[0]
    residual = error[0]
    experts_here, row_count, hidden = residual.shape
    rank_width = q_init.shape[1] // experts_here
    replicas = membership.shape[0]
    groups = GROUPS
    group_size = replicas // groups
    my_group = membership[lax.axis_index("dp")]
    group_mask = (jnp.arange(groups) == my_group).astype(jnp.float32)
    order = jnp.argsort(modality, stable=True)
    rank_of = jnp.argsort(order, stable=True)
    gradient = jnp.einsum("ktd,kth->kdh", tok_x, grads_out, preferred_element_type=jnp.float32)
    merged = (gradient + residual.astype(jnp.float32)).astype(jnp.bfloat16)
    q_blocks = q_init.reshape(hidden, experts_here, rank_width)
    left_part = jnp.einsum("kdh,hkr->dkr", merged, q_blocks, preferred_element_type=jnp.float32)
    left_part = left_part.reshape(row_count, experts_here * rank_width)
    image_part, text_part = split_columns(left_part, order, rank_width, group_mask)
    image_sum, text_slots = lax.psum((image_part, text_part), "dp")
    left_mean = join_columns(
        image_sum, text_slots, rank_of, group_mask, rank_width, replicas, group_size
    )
    blocks = left_mean.reshape(row_count, experts_here, rank_width)
    local_gram = jnp.einsum("dkr,dks->krs", blocks, blocks, precision=highest)
    gram_block = lax.psum(local_gram, "expert")
    identity = jnp.eye(rank_width, dtype=jnp.float32)
    shift_term = 0.001 * jnp.trace(gram_block, axis1=1, axis2=2) / rank_width
    factor_low = jnp.linalg.cholesky(gram_block + shift_term[:, None, None] * identity)
    inverse = jax.scipy.linalg.solve_triangular(
        factor_low, jnp.broadcast_to(identity, factor_low.shape), lower=True
    )
    p_hat = jnp.einsum("dkr,ksr->dks", blocks, inverse, precision=highest).astype(jnp.bfloat16)
    part_q = jnp.einsum("kdh,dkr->hkr", merged, p_hat, preferred_element_type=jnp.float32)
    q_local = part_q.reshape(hidden, experts_here * rank_width)
    image_part, text_part = split_columns(q_local, order, rank_width, group_mask)
    image_sum, text_slots = lax.psum((image_part, text_part), ("dp", "expert"))
    q_mean = join_columns(
        image_sum, text_slots, rank_of, group_mask, rank_width, replicas, group_size
    )
    q_sum = q_mean.astype(jnp.bfloat16)
    approx = jnp.einsum(
        "dkr,hkr->kdh",
        p_hat,
        q_sum.reshape(hidden, experts_here, rank_width),
        preferred_element_type=jnp.float32,
    )
    error_new = (merged.astype(jnp.float32) - approx).astype(jnp.bfloat16)
    return (q_sum[None], error_new[None])


MESH = pl.DeviceIdType.MESH
F32 = jnp.float32
BF16 = jnp.bfloat16


def compress_kernel(
    n_dp, n_ex, group_size,
    x_hbm, d_hbm, err_hbm, q_ref, modality, membership,
    merged_hbm, pt_out, qt_out,
    xs, ds, merged, lsend, lrecv, msend, lmean, gsend, grecv, pt_ref,
    qpart, qr1, qs2, qr2, q3, qr3, q4, qf,
    x_sem, d_sem, e_sem, m_sem, ls_sem, lr_sem, ms_sem, mr_sem, gs_sem, gr_sem,
    s1_sem, r1_sem, s2_sem, r2_sem, s3_sem, r3_sem, s4_sem, r4_sem,
    s5_sem, r5_sem,
):
    dp = lax.axis_index("dp")
    ex = lax.axis_index("expert")
    core, row = ex % 2, ex // 2
    ex_core = row * 2 + (1 - core)
    ex_row = (1 - row) * 2 + core
    ex_far = (1 - row) * 2 + (1 - core)
    experts, tokens, rows = xs.shape
    hidden = ds.shape[2]
    width = q_ref.shape[1]
    rank = width // experts
    step_rows = rows // n_dp
    slab = hidden // n_ex
    part = width // n_dp

    def remote(src, dst, send, recv, dp_to, ex_to):
        return pltpu.make_async_remote_copy(
            src_ref=src, dst_ref=dst, send_sem=send, recv_sem=recv,
            device_id=(dp_to, ex_to), device_id_type=MESH,
        )

    def rows_of(c, size):
        return pl.ds(pl.multiple_of(c * size, size), size)

    def err_copy(s):
        at = rows_of((dp + 1 + s) % n_dp, step_rows)
        return pltpu.make_async_copy(err_hbm.at[:, at, :], merged.at[:, at, :], e_sem.at[s])

    def merged_copy(s):
        at = rows_of((dp + 1 + s) % n_dp, step_rows)
        return pltpu.make_async_copy(merged.at[:, at, :], merged_hbm.at[:, at, :], m_sem.at[s])

    x_copies = [pltpu.make_async_copy(x_hbm.at[k], xs.at[k], x_sem.at[k]) for k in range(experts)]
    d_copies = [pltpu.make_async_copy(d_hbm.at[k], ds.at[k], d_sem.at[k]) for k in range(experts)]
    for k in range(experts):
        x_copies[k].start()
        d_copies[k].start()
    for s in range(n_dp):
        err_copy(s).start()

    barrier = pltpu.get_barrier_semaphore()
    for s in range(1, n_dp):
        pl.semaphore_signal(barrier, inc=1, device_id=((dp + s) % n_dp, ex), device_id_type=MESH)
    for other in (ex_core, ex_row, ex_far):
        pl.semaphore_signal(barrier, inc=1, device_id=(dp, other), device_id_type=MESH)
    pl.semaphore_wait(barrier, n_dp - 1 + 3)

    for k in range(experts):
        x_copies[k].wait()
        d_copies[k].wait()

    lane = lax.broadcasted_iota(jnp.int32, (1, width), 1)

    def left_copy(c, src):
        return remote(lsend.at[c], lrecv.at[src], ls_sem.at[c], lr_sem.at[src], c, ex)

    def left_step(s, carry):
        c = (dp + 1 + s) % n_dp
        at = rows_of(c, step_rows)
        err_copy(s).wait()
        total = jnp.zeros((step_rows, width), F32)
        for k in range(experts):
            xk = xs[k, :, at]
            mine = jnp.zeros((step_rows, width), F32)
            for n in range(3):
                cols = slice(n * (hidden // 3), (n + 1) * (hidden // 3))
                grad = lax.dot_general(
                    xk, ds[k, :, cols], (((0,), (0,)), ((), ())), preferred_element_type=F32
                )
                both = (grad + merged[k, at, cols].astype(F32)).astype(BF16)
                merged[k, at, cols] = both
                mine += jnp.dot(both, q_ref[cols, :], preferred_element_type=F32)
            total += jnp.where(lane // rank == k, mine, 0.0)
        merged_copy(s).start()

        @pl.when(s < n_dp - 1)
        def _():
            lsend[c] = total.astype(BF16)
            left_copy(c, dp).start()

        @pl.when(s == n_dp - 1)
        def _():
            lrecv[dp] = total.astype(BF16)

        return carry

    lax.fori_loop(0, n_dp, left_step, 0)

    def wait_left(s, carry):
        left_copy((dp + s) % n_dp, (dp + n_dp - s) % n_dp).wait_recv()
        return carry

    lax.fori_loop(1, n_dp, wait_left, 0)

    image = jnp.zeros((1, width), F32)
    for k in range(experts):
        flag = jnp.where(modality[k] == 0, 1.0, 0.0)
        image = jnp.where(lane // rank == k, flag, image)

    def mean_copy(i, src):
        return remote(msend.at[i], lmean.at[src], ms_sem.at[i], mr_sem.at[src], i, ex)

    def mean_step(s, carry):
        i = (dp + 1 + s) % n_dp
        acc = jnp.zeros((step_rows, width), F32)
        for j in range(n_dp):
            same = jnp.where(membership[i] == membership[j], 1.0 / group_size, 0.0)
            weight = jnp.where(image > 0.5, 1.0 / n_dp, same)
            acc += weight * lrecv[j].astype(F32)

        @pl.when(s < n_dp - 1)
        def _():
            msend[i] = acc.astype(BF16)
            mean_copy(i, dp).start()

        @pl.when(s == n_dp - 1)
        def _():
            lmean[dp] = acc.astype(BF16)

        return carry

    lax.fori_loop(0, n_dp, mean_step, 0)

    def gram_of(j):
        block = lmean[j]
        return lax.dot_general(block, block, (((0,), (0,)), ((), ())), preferred_element_type=F32)

    def gram_step(s, acc):
        j = (dp + n_dp - s) % n_dp
        mean_copy((dp + s) % n_dp, j).wait_recv()
        return acc + gram_of(j)

    gram = lax.fori_loop(1, n_dp, gram_step, gram_of(dp))
    pairs = experts // 2
    pair_lane = lax.broadcasted_iota(jnp.int32, (rank, 2 * rank), 1)
    pair_row = lax.broadcasted_iota(jnp.int32, (rank, 2 * rank), 0)
    low = pair_lane < rank
    for p in range(pairs):
        b = 2 * p * rank
        gsend[p] = jnp.where(
            low, gram[b : b + rank, b : b + 2 * rank], gram[b + rank : b + 2 * rank, b : b + 2 * rank]
        )
    grecv[ex] = gsend[...]
    others = (ex_core, ex_row, ex_far)
    gram_sends = [
        remote(gsend, grecv.at[ex], gs_sem.at[n], gr_sem.at[n], dp, other)
        for n, other in enumerate(others)
    ]
    for copy in gram_sends:
        copy.start()
    for n, other in enumerate(others):
        remote(gsend, grecv.at[other], gs_sem.at[n], gr_sem.at[n], dp, other).wait_recv()
    full = grecv[0]
    for e in range(1, n_ex):
        full = full + grecv[e]

    spots = (pair_lane == pair_row, pair_lane == pair_row + rank)
    work = []
    for odd in range(2):
        diag, unit = spots[odd], spots[1 - odd]
        trace = jnp.sum(jnp.where(diag, full, 0.0), axis=(1, 2), keepdims=True)
        a = full + jnp.where(diag, 0.001 * trace / rank, 0.0)
        here = low if odd == 0 else jnp.logical_not(low)
        work.append(jnp.where(here, a, jnp.where(unit, 1.0, 0.0)))
    done = [[], []]
    for j in range(rank):
        r = j % 8
        left_rows = rank - (j - r)
        below = lax.broadcasted_iota(jnp.int32, (1, left_rows, 1), 1) > r
        for odd in range(2):
            w = work[odd]
            at = j + odd * rank
            pivot = w[:, r : r + 1, :]
            scaled = pivot / w[:, r : r + 1, at : at + 1]
            work[odd] = w - jnp.where(below, w[:, :, at : at + 1], 0.0) * scaled
        if r == 7:
            for odd in range(2):
                done[odd].append(work[odd][:, :8, :])
                work[odd] = work[odd][:, 8:, :]
    blocks = []
    for p in range(pairs):
        for odd in range(2):
            w = jnp.concatenate([chunk[p] for chunk in done[odd]], axis=0)
            pivots = jnp.sum(jnp.where(spots[odd], w, 0.0), axis=1, keepdims=True)
            keep = jnp.logical_not(low) if odd == 0 else low
            inverse = jnp.where(keep, w, 0.0) / jnp.sqrt(pivots)
            inverse = pltpu.roll(inverse, rank, 1)
            zero = jnp.zeros((rank, 2 * rank), F32)
            blocks.append(
                jnp.concatenate([inverse if q == p else zero for q in range(pairs)], axis=1)
            )
    inv = jnp.concatenate(blocks, axis=0)
    inv_high = inv.astype(BF16)
    inv_low = (inv - inv_high.astype(F32)).astype(BF16)
    for j in range(n_dp):
        block = lmean[j]
        dims = (((1,), (1,)), ((), ()))
        p_t = lax.dot_general(inv_high, block, dims, preferred_element_type=F32)
        p_t += lax.dot_general(inv_low, block, dims, preferred_element_type=F32)
        pt_ref[:, j * step_rows : (j + 1) * step_rows] = p_t.astype(BF16)
    pt_out[...] = pt_ref[...]

    def k_rows(k):
        return pl.ds(k * rank, rank)

    def core_copy(k, n):
        slab_at = (ex_core, ex_far)[n]
        return remote(
            qpart.at[slab_at, k_rows(k), :], qr1.at[n, k_rows(k), :],
            s1_sem.at[n, k], r1_sem.at[n, k], dp, ex_core,
        )

    def row_copy(k):
        return remote(
            qs2.at[k_rows(k), :], qr2.at[k_rows(k), :], s2_sem.at[k], r2_sem.at[k], dp, ex_row
        )

    def part_copy(c, src):
        return remote(
            q3.at[rows_of(c, part), :], qr3.at[src], s3_sem.at[c], r3_sem.at[src], c, ex
        )

    per = rank // part

    def stage_one(k):
        p_k = pt_ref[k * rank : (k + 1) * rank, :]
        for e in range(n_ex):
            out = jnp.dot(
                p_k, merged[k, :, e * slab : (e + 1) * slab], preferred_element_type=F32
            )
            qpart[e, k * rank : (k + 1) * rank, :] = out.astype(BF16)
        core_copy(k, 1).start()
        core_copy(k, 0).start()

    def stage_two(k):
        core_copy(k, 1).wait_recv()
        at = slice(k * rank, (k + 1) * rank)
        qs2[at, :] = (qpart[ex_row, at, :].astype(F32) + qr1[1, at, :].astype(F32)).astype(BF16)
        row_copy(k).start()

    def stage_three(k):
        core_copy(k, 0).wait_recv()
        row_copy(k).wait_recv()
        at = slice(k * rank, (k + 1) * rank)
        q3[at, :] = (
            qpart[ex, at, :].astype(F32) + qr1[0, at, :].astype(F32) + qr2[at, :].astype(F32)
        ).astype(BF16)
        for c in range(k * per, (k + 1) * per):

            @pl.when(dp != c)
            def _():
                part_copy(c, dp).start()

            @pl.when(dp == c)
            def _():
                qr3[c] = q3[c * part : (c + 1) * part, :]

    for k in range(experts + 2):
        if k < experts:
            stage_one(k)
        if 1 <= k <= experts:
            stage_two(k - 1)
        if k >= 2:
            stage_three(k - 2)

    def wait_part(s, carry):
        part_copy((dp + s) % n_dp, (dp + n_dp - s) % n_dp).wait_recv()
        return carry

    lax.fori_loop(1, n_dp, wait_part, 0)
    my_image = modality[dp // per] == 0

    def back_copy(i, src):
        return remote(
            q4.at[i], qf.at[ex, rows_of(src, part), :], s4_sem.at[i], r4_sem.at[src], i, ex
        )

    def back_step(s, carry):
        i = (dp + 1 + s) % n_dp
        acc = jnp.zeros((part, slab), F32)
        for j in range(n_dp):
            same = jnp.where(membership[i] == membership[j], 1.0 / group_size, 0.0)
            acc += jnp.where(my_image, 1.0 / n_dp, same) * qr3[j].astype(F32)

        @pl.when(s < n_dp - 1)
        def _():
            q4[i] = acc.astype(BF16)
            back_copy(i, dp).start()

        @pl.when(s == n_dp - 1)
        def _():
            qf[ex, rows_of(dp, part), :] = acc.astype(BF16)

        return carry

    lax.fori_loop(0, n_dp, back_step, 0)

    def spread(c, n):
        held, to = ((ex, ex_core), (ex, ex_row), (ex_row, ex_core))[n]
        at = rows_of(c, part)
        return remote(
            qf.at[held, at, :], qf.at[held, at, :], s5_sem.at[n, c], r5_sem.at[n, c], dp, to
        )

    def spread_step(s, carry):
        c = (dp + n_dp - s) % n_dp

        @pl.when(s > 0)
        def _():
            back_copy((dp + s) % n_dp, c).wait_recv()

        spread(c, 1).start()
        spread(c, 0).start()
        return carry

    lax.fori_loop(0, n_dp, spread_step, 0)

    def forward_step(s, carry):
        c = (dp + n_dp - s) % n_dp
        spread(c, 1).wait_recv()
        spread(c, 2).start()
        return carry

    lax.fori_loop(0, n_dp, forward_step, 0)

    def last_step(s, carry):
        c = (dp + n_dp - s) % n_dp
        spread(c, 0).wait_recv()
        spread(c, 2).wait_recv()
        return carry

    lax.fori_loop(0, n_dp, last_step, 0)
    for e in range(n_ex):
        qt_out[:, e * slab : (e + 1) * slab] = qf[e]

    def drain(s, carry):
        i = (dp + s) % n_dp
        left_copy(i, dp).wait_send()
        mean_copy(i, dp).wait_send()
        part_copy(i, dp).wait_send()
        back_copy(i, dp).wait_send()
        return carry

    lax.fori_loop(1, n_dp, drain, 0)

    def drain_all(c, carry):
        for n in range(3):
            spread(c, n).wait_send()
        merged_copy(c).wait()
        return carry

    lax.fori_loop(0, n_dp, drain_all, 0)
    for k in range(experts):
        core_copy(k, 0).wait_send()
        core_copy(k, 1).wait_send()
        row_copy(k).wait_send()
    for copy in gram_sends:
        copy.wait_send()


def residual_kernel(pt_ref, qt_ref, merged_ref, out_ref):
    approx = lax.dot_general(
        pt_ref[...], qt_ref[...], (((0,), (0,)), ((), ())), preferred_element_type=F32
    )
    out_ref[0] = (merged_ref[0].astype(F32) - approx).astype(BF16)


def tiled_form(n_dp, n_ex, x_act, d_out, error, q_init, modality, membership):
    experts, tokens, rows = x_act.shape[1:]
    hidden = d_out.shape[3]
    width = q_init.shape[1]
    rank = width // experts
    slab, part, step_rows = hidden // n_ex, width // n_dp, rows // n_dp
    group_size = membership.shape[0] // GROUPS
    any_spec = pl.BlockSpec(memory_space=pl.ANY)
    vmem = pl.BlockSpec(memory_space=pltpu.VMEM)
    smem = pl.BlockSpec(memory_space=pltpu.SMEM)
    dma = pltpu.SemaphoreType.DMA
    merged, p_t, q_t = pl.pallas_call(
        functools.partial(compress_kernel, n_dp, n_ex, group_size),
        out_shape=(
            jax.ShapeDtypeStruct((experts, rows, hidden), BF16),
            jax.ShapeDtypeStruct((width, rows), BF16),
            jax.ShapeDtypeStruct((width, hidden), BF16),
        ),
        in_specs=[any_spec, any_spec, any_spec, vmem, smem, smem],
        out_specs=(any_spec, vmem, vmem),
        scratch_shapes=[
            pltpu.VMEM((experts, tokens, rows), BF16),
            pltpu.VMEM((experts, tokens, hidden), BF16),
            pltpu.VMEM((experts, rows, hidden), BF16),
            pltpu.VMEM((n_dp, step_rows, width), BF16),
            pltpu.VMEM((n_dp, step_rows, width), BF16),
            pltpu.VMEM((n_dp, step_rows, width), BF16),
            pltpu.VMEM((n_dp, step_rows, width), BF16),
            pltpu.VMEM((experts // 2, rank, 2 * rank), F32),
            pltpu.VMEM((n_ex, experts // 2, rank, 2 * rank), F32),
            pltpu.VMEM((width, rows), BF16),
            pltpu.VMEM((n_ex, width, slab), BF16),
            pltpu.VMEM((2, width, slab), BF16),
            pltpu.VMEM((width, slab), BF16),
            pltpu.VMEM((width, slab), BF16),
            pltpu.VMEM((width, slab), BF16),
            pltpu.VMEM((n_dp, part, slab), BF16),
            pltpu.VMEM((n_dp, part, slab), BF16),
            pltpu.VMEM((n_ex, width, slab), BF16),
            dma((experts,)), dma((experts,)), dma((n_dp,)), dma((n_dp,)),
            dma((n_dp,)), dma((n_dp,)), dma((n_dp,)), dma((n_dp,)),
            dma((3,)), dma((3,)),
            dma((2, experts)), dma((2, experts)), dma((experts,)), dma((experts,)),
            dma((n_dp,)), dma((n_dp,)), dma((n_dp,)), dma((n_dp,)),
            dma((3, n_dp)), dma((3, n_dp)),
        ],
        compiler_params=pltpu.CompilerParams(
            collective_id=0, has_side_effects=True, vmem_limit_bytes=50 * 2**20
        ),
        cost_estimate=pl.CostEstimate(
            flops=12 * experts * rows * hidden * tokens // 4,
            bytes_accessed=4 * experts * rows * hidden,
            transcendentals=0,
        ),
        name="compress",
    )(x_act[0], d_out[0], error[0], q_init, modality, membership)
    block = rows // 4
    error_new = pl.pallas_call(
        residual_kernel,
        grid=(experts, rows // block),
        out_shape=jax.ShapeDtypeStruct((experts, rows, hidden), BF16),
        in_specs=[
            pl.BlockSpec((rank, block), lambda k, r: (k, r)),
            pl.BlockSpec((rank, hidden), lambda k, r: (k, 0)),
            pl.BlockSpec((1, block, hidden), lambda k, r: (k, r, 0)),
        ],
        out_specs=pl.BlockSpec((1, block, hidden), lambda k, r: (k, r, 0)),
        compiler_params=pltpu.CompilerParams(vmem_limit_bytes=32 * 2**20),
        name="residual",
    )(p_t, q_t, merged)
    return (q_t.T[None], error_new[None])


def tiles(n_dp, n_ex, x_act, d_out, error, q_init, modality, membership):
    experts, _, rows = x_act.shape[1:]
    hidden, width = q_init.shape
    rank = width // experts
    return (
        n_ex == 4
        and experts % 2 == 0
        and 2 * rank == 128
        and experts % 2 == 0
        and rank % (width // n_dp) == 0
        and (width // n_dp) % 16 == 0
        and (rows // n_dp) % 128 == 0
        and (hidden // n_ex) % 128 == 0
        and (hidden // 3) % 128 == 0
    )


def solution(mesh):
    in_specs = (
        P("dp", None, None, "expert"),
        P("dp", None, None, None),
        P("dp", None, "expert", None),
        P(),
        P(),
        P(),
    )
    out_specs = (P("dp", None, None), P("dp", None, "expert", None))
    n_dp, n_ex = mesh.shape["dp"], mesh.shape["expert"]

    def body(*args):
        if tiles(n_dp, n_ex, *args):
            return tiled_form(n_dp, n_ex, *args)
        return on_device(*args)

    return jax.shard_map(
        body, mesh=mesh, in_specs=in_specs, out_specs=out_specs, check_vma=False
    )
```

```python
import functools

import jax
import jax.numpy as jnp
from jax import lax
from jax.experimental import pallas as pl
from jax.experimental.pallas import tpu as pltpu
from jax.sharding import PartitionSpec as P

GROUPS = 4


highest = lax.Precision.HIGHEST


def split_columns(values, order, rank_width, group_mask):
    count = values.shape[0]
    experts_here = order.shape[0]
    half = experts_here // 2
    taken = jnp.take(values.reshape(count, experts_here, rank_width), order, axis=1)
    image_part = taken[:, :half].reshape(count, half * rank_width)
    text_part = taken[:, half:].reshape(count, half * rank_width)
    return (image_part, group_mask[:, None, None] * text_part)


def join_columns(image_sum, text_slots, rank_of, group_mask, rank_width, replicas, group_size):
    count = image_sum.shape[0]
    half = image_sum.shape[1] // rank_width
    image_mean = (image_sum / replicas).reshape(count, half, rank_width)
    text_mean = (jnp.sum(group_mask[:, None, None] * text_slots, axis=0) / group_size).reshape(
        count, half, rank_width
    )
    joined = jnp.concatenate([image_mean, text_mean], axis=1)
    return jnp.take(joined, rank_of, axis=1).reshape(count, 2 * half * rank_width)


def on_device(x_act, d_out, error, q_init, modality, membership):
    tok_x = x_act[0]
    grads_out = d_out[0]
    residual = error[0]
    experts_here, row_count, hidden = residual.shape
    rank_width = q_init.shape[1] // experts_here
    replicas = membership.shape[0]
    groups = GROUPS
    group_size = replicas // groups
    my_group = membership[lax.axis_index("dp")]
    group_mask = (jnp.arange(groups) == my_group).astype(jnp.float32)
    order = jnp.argsort(modality, stable=True)
    rank_of = jnp.argsort(order, stable=True)
    gradient = jnp.einsum("ktd,kth->kdh", tok_x, grads_out, preferred_element_type=jnp.float32)
    merged = (gradient + residual.astype(jnp.float32)).astype(jnp.bfloat16)
    q_blocks = q_init.reshape(hidden, experts_here, rank_width)
    left_part = jnp.einsum("kdh,hkr->dkr", merged, q_blocks, preferred_element_type=jnp.float32)
    left_part = left_part.reshape(row_count, experts_here * rank_width)
    image_part, text_part = split_columns(left_part, order, rank_width, group_mask)
    image_sum, text_slots = lax.psum((image_part, text_part), "dp")
    left_mean = join_columns(
        image_sum, text_slots, rank_of, group_mask, rank_width, replicas, group_size
    )
    blocks = left_mean.reshape(row_count, experts_here, rank_width)
    local_gram = jnp.einsum("dkr,dks->krs", blocks, blocks, precision=highest)
    gram_block = lax.psum(local_gram, "expert")
    identity = jnp.eye(rank_width, dtype=jnp.float32)
    shift_term = 0.001 * jnp.trace(gram_block, axis1=1, axis2=2) / rank_width
    factor_low = jnp.linalg.cholesky(gram_block + shift_term[:, None, None] * identity)
    inverse = jax.scipy.linalg.solve_triangular(
        factor_low, jnp.broadcast_to(identity, factor_low.shape), lower=True
    )
    p_hat = jnp.einsum("dkr,ksr->dks", blocks, inverse, precision=highest).astype(jnp.bfloat16)
    part_q = jnp.einsum("kdh,dkr->hkr", merged, p_hat, preferred_element_type=jnp.float32)
    q_local = part_q.reshape(hidden, experts_here * rank_width)
    image_part, text_part = split_columns(q_local, order, rank_width, group_mask)
    image_sum, text_slots = lax.psum((image_part, text_part), ("dp", "expert"))
    q_mean = join_columns(
        image_sum, text_slots, rank_of, group_mask, rank_width, replicas, group_size
    )
    q_sum = q_mean.astype(jnp.bfloat16)
    approx = jnp.einsum(
        "dkr,hkr->kdh",
        p_hat,
        q_sum.reshape(hidden, experts_here, rank_width),
        preferred_element_type=jnp.float32,
    )
    error_new = (merged.astype(jnp.float32) - approx).astype(jnp.bfloat16)
    return (q_sum[None], error_new[None])


MESH = pl.DeviceIdType.MESH
F32 = jnp.float32
BF16 = jnp.bfloat16


def compress_kernel(
    n_dp, n_ex, group_size,
    x_hbm, d_hbm, err_hbm, q_hbm, modality_hbm, membership_hbm,
    merged_hbm, pt_ref, qt_out,
    q_ref, modality, membership, xs, ds, merged, lsend, lrecv, msend, lmean, gsend, grecv,
    qpart, qr1, qs2, qr2, q3, qr3, q4, qf,
    in_sem, x_sem, d_sem, e_sem, m_sem, ls_sem, lr_sem, ms_sem, mr_sem, gs_sem, gr_sem,
    s1_sem, r1_sem, s2_sem, r2_sem, s3_sem, r3_sem, s4_sem, r4_sem,
    s5_sem, r5_sem,
):
    dp = lax.axis_index("dp")
    ex = lax.axis_index("expert")
    core, row = ex % 2, ex // 2
    ex_core = row * 2 + (1 - core)
    ex_row = (1 - row) * 2 + core
    ex_far = (1 - row) * 2 + (1 - core)
    experts, tokens, rows = xs.shape
    hidden = ds.shape[2]
    width = q_ref.shape[1]
    rank = width // experts
    step_rows = rows // n_dp
    slab = hidden // n_ex
    part = width // n_dp

    def remote(src, dst, send, recv, dp_to, ex_to):
        return pltpu.make_async_remote_copy(
            src_ref=src, dst_ref=dst, send_sem=send, recv_sem=recv,
            device_id=(dp_to, ex_to), device_id_type=MESH,
        )

    def rows_of(c, size):
        return pl.ds(pl.multiple_of(c * size, size), size)

    twos = n_dp // 2
    two_rows = 2 * step_rows

    def two_of(s):
        return (dp // 2 + 1 + s) % twos

    def err_copy(s):
        at = rows_of(two_of(s), two_rows)
        return pltpu.make_async_copy(err_hbm.at[:, at, :], merged.at[:, at, :], e_sem.at[s])

    def merged_copy(s):
        at = rows_of(two_of(s), two_rows)
        return pltpu.make_async_copy(merged.at[:, at, :], merged_hbm.at[:, at, :], m_sem.at[s])

    x_copies = [pltpu.make_async_copy(x_hbm.at[k], xs.at[k], x_sem.at[k]) for k in range(experts)]
    d_copies = [pltpu.make_async_copy(d_hbm.at[k], ds.at[k], d_sem.at[k]) for k in range(experts)]
    for k in range(experts):
        x_copies[k].start()
        d_copies[k].start()
    small = [
        pltpu.make_async_copy(src, dst, in_sem.at[n])
        for n, (src, dst) in enumerate(
            ((q_hbm, q_ref), (modality_hbm, modality), (membership_hbm, membership))
        )
    ]
    for copy in small:
        copy.start()
    for s in range(twos):
        err_copy(s).start()

    barrier = pltpu.get_barrier_semaphore()
    for s in range(1, n_dp):
        pl.semaphore_signal(barrier, inc=1, device_id=((dp + s) % n_dp, ex), device_id_type=MESH)
    for other in (ex_core, ex_row, ex_far):
        pl.semaphore_signal(barrier, inc=1, device_id=(dp, other), device_id_type=MESH)
    pl.semaphore_wait(barrier, n_dp - 1 + 3)

    for k in range(experts):
        x_copies[k].wait()
        d_copies[k].wait()
    for copy in small:
        copy.wait()

    lane = lax.broadcasted_iota(jnp.int32, (1, width), 1)

    def left_copy(c, src):
        return remote(lsend.at[c], lrecv.at[src], ls_sem.at[c], lr_sem.at[src], c, ex)

    def left_step(s, carry):
        two = two_of(s)
        at = rows_of(two, two_rows)
        err_copy(s).wait()
        total = jnp.zeros((two_rows, width), F32)
        for k in range(experts):
            xk = xs[k, :, at]
            mine = jnp.zeros((two_rows, width), F32)
            for n in range(3):
                cols = slice(n * (hidden // 3), (n + 1) * (hidden // 3))
                grad = lax.dot_general(
                    xk, ds[k, :, cols], (((0,), (0,)), ((), ())), preferred_element_type=F32
                )
                both = (grad + merged[k, at, cols].astype(F32)).astype(BF16)
                merged[k, at, cols] = both
                mine += jnp.dot(both, q_ref[cols, :], preferred_element_type=F32)
            total += jnp.where(lane // rank == k, mine, 0.0)
        merged_copy(s).start()
        for h in range(2):
            c = 2 * two + h
            block = total[h * step_rows : (h + 1) * step_rows, :].astype(BF16)

            @pl.when(c != dp)
            def _():
                lsend[c] = block
                left_copy(c, dp).start()

            @pl.when(c == dp)
            def _():
                lrecv[dp] = block

        return carry

    lax.fori_loop(0, twos, left_step, 0)

    def wait_left(s, carry):
        left_copy((dp + s) % n_dp, (dp + n_dp - s) % n_dp).wait_recv()
        return carry

    lax.fori_loop(1, n_dp, wait_left, 0)

    image = jnp.zeros((1, width), F32)
    for k in range(experts):
        flag = jnp.where(modality[k] == 0, 1.0, 0.0)
        image = jnp.where(lane // rank == k, flag, image)

    def mean_copy(i, src):
        return remote(msend.at[i], lmean.at[src], ms_sem.at[i], mr_sem.at[src], i, ex)

    def mean_step(s, carry):
        i = (dp + 1 + s) % n_dp
        acc = jnp.zeros((step_rows, width), F32)
        for j in range(n_dp):
            same = jnp.where(membership[i] == membership[j], 1.0 / group_size, 0.0)
            weight = jnp.where(image > 0.5, 1.0 / n_dp, same)
            acc += weight * lrecv[j].astype(F32)

        @pl.when(s < n_dp - 1)
        def _():
            msend[i] = acc.astype(BF16)
            mean_copy(i, dp).start()

        @pl.when(s == n_dp - 1)
        def _():
            lmean[dp] = acc.astype(BF16)

        return carry

    lax.fori_loop(0, n_dp, mean_step, 0)

    def gram_of(j):
        block = lmean[j]
        return lax.dot_general(block, block, (((0,), (0,)), ((), ())), preferred_element_type=F32)

    def gram_step(s, acc):
        j = (dp + n_dp - s) % n_dp
        mean_copy((dp + s) % n_dp, j).wait_recv()
        return acc + gram_of(j)

    gram = lax.fori_loop(1, n_dp, gram_step, gram_of(dp))
    pairs = experts // 2
    pair_lane = lax.broadcasted_iota(jnp.int32, (rank, 2 * rank), 1)
    pair_row = lax.broadcasted_iota(jnp.int32, (rank, 2 * rank), 0)
    low = pair_lane < rank
    for p in range(pairs):
        b = 2 * p * rank
        gsend[p] = jnp.where(
            low, gram[b : b + rank, b : b + 2 * rank], gram[b + rank : b + 2 * rank, b : b + 2 * rank]
        )
    grecv[ex] = gsend[...]
    others = (ex_core, ex_row, ex_far)
    gram_sends = [
        remote(gsend, grecv.at[ex], gs_sem.at[n], gr_sem.at[n], dp, other)
        for n, other in enumerate(others)
    ]
    for copy in gram_sends:
        copy.start()
    for n, other in enumerate(others):
        remote(gsend, grecv.at[other], gs_sem.at[n], gr_sem.at[n], dp, other).wait_recv()
    full = grecv[0]
    for e in range(1, n_ex):
        full = full + grecv[e]

    spots = (pair_lane == pair_row, pair_lane == pair_row + rank)
    work = []
    for odd in range(2):
        diag, unit = spots[odd], spots[1 - odd]
        trace = jnp.sum(jnp.where(diag, full, 0.0), axis=(1, 2), keepdims=True)
        a = full + jnp.where(diag, 0.001 * trace / rank, 0.0)
        here = low if odd == 0 else jnp.logical_not(low)
        work.append(jnp.where(here, a, jnp.where(unit, 1.0, 0.0)))
    done = [[], []]
    for j in range(rank):
        r = j % 8
        left_rows = rank - (j - r)
        below = lax.broadcasted_iota(jnp.int32, (1, left_rows, 1), 1) > r
        for odd in range(2):
            w = work[odd]
            at = j + odd * rank
            pivot = w[:, r : r + 1, :]
            scaled = pivot / w[:, r : r + 1, at : at + 1]
            work[odd] = w - jnp.where(below, w[:, :, at : at + 1], 0.0) * scaled
        if r == 7:
            for odd in range(2):
                done[odd].append(work[odd][:, :8, :])
                work[odd] = work[odd][:, 8:, :]
    blocks = []
    for p in range(pairs):
        for odd in range(2):
            w = jnp.concatenate([chunk[p] for chunk in done[odd]], axis=0)
            pivots = jnp.sum(jnp.where(spots[odd], w, 0.0), axis=1, keepdims=True)
            keep = jnp.logical_not(low) if odd == 0 else low
            inverse = jnp.where(keep, w, 0.0) / jnp.sqrt(pivots)
            inverse = pltpu.roll(inverse, rank, 1)
            zero = jnp.zeros((rank, 2 * rank), F32)
            blocks.append(
                jnp.concatenate([inverse if q == p else zero for q in range(pairs)], axis=1)
            )
    inv = jnp.concatenate(blocks, axis=0)
    inv_high = inv.astype(BF16)
    inv_low = (inv - inv_high.astype(F32)).astype(BF16)
    for j in range(n_dp):
        block = lmean[j]
        dims = (((1,), (1,)), ((), ()))
        p_t = lax.dot_general(inv_high, block, dims, preferred_element_type=F32)
        p_t += lax.dot_general(inv_low, block, dims, preferred_element_type=F32)
        pt_ref[:, j * step_rows : (j + 1) * step_rows] = p_t.astype(BF16)

    def k_rows(k):
        return pl.ds(k * rank, rank)

    def core_copy(k, n):
        slab_at = (ex_core, ex_far)[n]
        return remote(
            qpart.at[slab_at, k_rows(k), :], qr1.at[n, k_rows(k), :],
            s1_sem.at[n, k], r1_sem.at[n, k], dp, ex_core,
        )

    def row_copy(k):
        return remote(
            qs2.at[k_rows(k), :], qr2.at[k_rows(k), :], s2_sem.at[k], r2_sem.at[k], dp, ex_row
        )

    def part_copy(c, src):
        return remote(
            q3.at[rows_of(c, part), :], qr3.at[src], s3_sem.at[c], r3_sem.at[src], c, ex
        )

    per = rank // part

    def stage_one(k):
        p_k = pt_ref[k * rank : (k + 1) * rank, :]
        for e in range(n_ex):
            out = jnp.dot(
                p_k, merged[k, :, e * slab : (e + 1) * slab], preferred_element_type=F32
            )
            qpart[e, k * rank : (k + 1) * rank, :] = out.astype(BF16)
        core_copy(k, 1).start()
        core_copy(k, 0).start()

    def stage_two(k):
        core_copy(k, 1).wait_recv()
        at = slice(k * rank, (k + 1) * rank)
        qs2[at, :] = (qpart[ex_row, at, :].astype(F32) + qr1[1, at, :].astype(F32)).astype(BF16)
        row_copy(k).start()

    def stage_three(k):
        core_copy(k, 0).wait_recv()
        row_copy(k).wait_recv()
        at = slice(k * rank, (k + 1) * rank)
        q3[at, :] = (
            qpart[ex, at, :].astype(F32) + qr1[0, at, :].astype(F32) + qr2[at, :].astype(F32)
        ).astype(BF16)
        for c in range(k * per, (k + 1) * per):

            @pl.when(dp != c)
            def _():
                part_copy(c, dp).start()

            @pl.when(dp == c)
            def _():
                qr3[c] = q3[c * part : (c + 1) * part, :]

    for k in range(experts + 2):
        if k < experts:
            stage_one(k)
        if 1 <= k <= experts:
            stage_two(k - 1)
        if k >= 2:
            stage_three(k - 2)

    def wait_part(s, carry):
        part_copy((dp + s) % n_dp, (dp + n_dp - s) % n_dp).wait_recv()
        return carry

    lax.fori_loop(1, n_dp, wait_part, 0)
    my_image = modality[dp // per] == 0

    def back_copy(i, src):
        return remote(
            q4.at[i], qf.at[ex, rows_of(src, part), :], s4_sem.at[i], r4_sem.at[src], i, ex
        )

    def back_step(s, carry):
        i = (dp + 1 + s) % n_dp
        acc = jnp.zeros((part, slab), F32)
        for j in range(n_dp):
            same = jnp.where(membership[i] == membership[j], 1.0 / group_size, 0.0)
            acc += jnp.where(my_image, 1.0 / n_dp, same) * qr3[j].astype(F32)

        @pl.when(s < n_dp - 1)
        def _():
            q4[i] = acc.astype(BF16)
            back_copy(i, dp).start()

        @pl.when(s == n_dp - 1)
        def _():
            qf[ex, rows_of(dp, part), :] = acc.astype(BF16)

        return carry

    lax.fori_loop(0, n_dp, back_step, 0)

    def spread(c, n):
        held, to = ((ex, ex_core), (ex, ex_row), (ex_row, ex_core))[n]
        at = rows_of(c, part)
        return remote(
            qf.at[held, at, :], qf.at[held, at, :], s5_sem.at[n, c], r5_sem.at[n, c], dp, to
        )

    def spread_step(s, carry):
        c = (dp + n_dp - s) % n_dp

        @pl.when(s > 0)
        def _():
            back_copy((dp + s) % n_dp, c).wait_recv()

        spread(c, 1).start()
        spread(c, 0).start()
        return carry

    lax.fori_loop(0, n_dp, spread_step, 0)

    def forward_step(s, carry):
        c = (dp + n_dp - s) % n_dp
        spread(c, 1).wait_recv()
        spread(c, 2).start()
        return carry

    lax.fori_loop(0, n_dp, forward_step, 0)

    def last_step(s, carry):
        c = (dp + n_dp - s) % n_dp
        spread(c, 0).wait_recv()
        spread(c, 2).wait_recv()
        return carry

    lax.fori_loop(0, n_dp, last_step, 0)
    for e in range(n_ex):
        qt_out[:, e * slab : (e + 1) * slab] = qf[e]

    def drain(s, carry):
        i = (dp + s) % n_dp
        left_copy(i, dp).wait_send()
        mean_copy(i, dp).wait_send()
        part_copy(i, dp).wait_send()
        back_copy(i, dp).wait_send()
        return carry

    lax.fori_loop(1, n_dp, drain, 0)

    def drain_all(c, carry):
        for n in range(3):
            spread(c, n).wait_send()
        return carry

    lax.fori_loop(0, n_dp, drain_all, 0)
    for s in range(twos):
        merged_copy(s).wait()
    for k in range(experts):
        core_copy(k, 0).wait_send()
        core_copy(k, 1).wait_send()
        row_copy(k).wait_send()
    for copy in gram_sends:
        copy.wait_send()


def residual_kernel(
    pt_ref, qt_ref, merged, err_hbm, q_hbm, stage, q_stage, m_sem, e_sem, q_sem
):
    experts, rows, hidden = merged.shape
    rank = pt_ref.shape[0] // experts
    pieces, size = stage.shape[:2]
    per = rows // size

    def place(ref, t):
        return ref.at[t // per, pl.ds(pl.multiple_of((t % per) * size, size), size), :]

    def load(t):
        return pltpu.make_async_copy(place(merged, t), stage.at[t], m_sem.at[t])

    def copy(t):
        return pltpu.make_async_copy(stage.at[t], place(err_hbm, t), e_sem.at[t])

    for t in range(pieces):
        load(t).start()

    def step(t, carry):
        at = pl.ds(pl.multiple_of((t % per) * size, size), size)
        of = pl.ds(pl.multiple_of((t // per) * rank, rank), rank)
        approx = lax.dot_general(
            pt_ref[of, at], qt_ref[of, :], (((0,), (0,)), ((), ())), preferred_element_type=F32
        )
        load(t).wait()
        stage[t] = (stage[t].astype(F32) - approx).astype(BF16)
        copy(t).start()
        return carry

    lax.fori_loop(0, pieces, step, 0)
    q_stage[...] = qt_ref[...].T
    q_copy = pltpu.make_async_copy(q_stage, q_hbm, q_sem)
    q_copy.start()

    def wait(t, carry):
        copy(t).wait()
        return carry

    lax.fori_loop(0, pieces, wait, 0)
    q_copy.wait()


def tiled_form(n_dp, n_ex, x_act, d_out, error, q_init, modality, membership):
    experts, tokens, rows = x_act.shape[1:]
    hidden = d_out.shape[3]
    width = q_init.shape[1]
    rank = width // experts
    slab, part, step_rows = hidden // n_ex, width // n_dp, rows // n_dp
    group_size = membership.shape[0] // GROUPS
    any_spec = pl.BlockSpec(memory_space=pl.ANY)
    vmem = pl.BlockSpec(memory_space=pltpu.VMEM)
    dma = pltpu.SemaphoreType.DMA
    merged, p_t, q_t = pl.pallas_call(
        functools.partial(compress_kernel, n_dp, n_ex, group_size),
        out_shape=(
            jax.ShapeDtypeStruct((experts, rows, hidden), BF16),
            jax.ShapeDtypeStruct((width, rows), BF16),
            jax.ShapeDtypeStruct((width, hidden), BF16),
        ),
        in_specs=[any_spec] * 6,
        out_specs=(any_spec, vmem, vmem),
        scratch_shapes=[
            pltpu.VMEM((hidden, width), BF16),
            pltpu.SMEM(modality.shape, jnp.int32),
            pltpu.SMEM(membership.shape, jnp.int32),
            pltpu.VMEM((experts, tokens, rows), BF16),
            pltpu.VMEM((experts, tokens, hidden), BF16),
            pltpu.VMEM((experts, rows, hidden), BF16),
            pltpu.VMEM((n_dp, step_rows, width), BF16),
            pltpu.VMEM((n_dp, step_rows, width), BF16),
            pltpu.VMEM((n_dp, step_rows, width), BF16),
            pltpu.VMEM((n_dp, step_rows, width), BF16),
            pltpu.VMEM((experts // 2, rank, 2 * rank), F32),
            pltpu.VMEM((n_ex, experts // 2, rank, 2 * rank), F32),
            pltpu.VMEM((n_ex, width, slab), BF16),
            pltpu.VMEM((2, width, slab), BF16),
            pltpu.VMEM((width, slab), BF16),
            pltpu.VMEM((width, slab), BF16),
            pltpu.VMEM((width, slab), BF16),
            pltpu.VMEM((n_dp, part, slab), BF16),
            pltpu.VMEM((n_dp, part, slab), BF16),
            pltpu.VMEM((n_ex, width, slab), BF16),
            dma((3,)), dma((experts,)), dma((experts,)), dma((n_dp // 2,)), dma((n_dp // 2,)),
            dma((n_dp,)), dma((n_dp,)), dma((n_dp,)), dma((n_dp,)),
            dma((3,)), dma((3,)),
            dma((2, experts)), dma((2, experts)), dma((experts,)), dma((experts,)),
            dma((n_dp,)), dma((n_dp,)), dma((n_dp,)), dma((n_dp,)),
            dma((3, n_dp)), dma((3, n_dp)),
        ],
        compiler_params=pltpu.CompilerParams(
            collective_id=0, has_side_effects=True, vmem_limit_bytes=56 * 2**20
        ),
        cost_estimate=pl.CostEstimate(
            flops=12 * experts * rows * hidden * tokens // 4,
            bytes_accessed=4 * experts * rows * hidden,
            transcendentals=0,
        ),
        name="compress",
    )(x_act[0], d_out[0], error[0], q_init, modality, membership)
    block = rows // 4
    error_new, q_sum = pl.pallas_call(
        residual_kernel,
        out_shape=(
            jax.ShapeDtypeStruct((experts, rows, hidden), BF16),
            jax.ShapeDtypeStruct((hidden, width), BF16),
        ),
        in_specs=[vmem, vmem, any_spec],
        out_specs=(any_spec, any_spec),
        scratch_shapes=[
            pltpu.VMEM((experts * rows // block, block, hidden), BF16),
            pltpu.VMEM((hidden, width), BF16),
            dma((experts * rows // block,)),
            dma((experts * rows // block,)),
            dma,
        ],
        compiler_params=pltpu.CompilerParams(vmem_limit_bytes=56 * 2**20),
        name="residual",
    )(p_t, q_t, merged)
    return (q_sum[None], error_new[None])


def tiles(n_dp, n_ex, x_act, d_out, error, q_init, modality, membership):
    experts, _, rows = x_act.shape[1:]
    hidden, width = q_init.shape
    rank = width // experts
    return (
        n_ex == 4
        and experts % 2 == 0
        and 2 * rank == 128
        and experts % 2 == 0
        and rank % (width // n_dp) == 0
        and (width // n_dp) % 16 == 0
        and (rows // n_dp) % 128 == 0
        and (hidden // n_ex) % 128 == 0
        and (hidden // 3) % 128 == 0
    )


def solution(mesh):
    in_specs = (
        P("dp", None, None, "expert"),
        P("dp", None, None, None),
        P("dp", None, "expert", None),
        P(),
        P(),
        P(),
    )
    out_specs = (P("dp", None, None), P("dp", None, "expert", None))
    n_dp, n_ex = mesh.shape["dp"], mesh.shape["expert"]

    def body(*args):
        if tiles(n_dp, n_ex, *args):
            return tiled_form(n_dp, n_ex, *args)
        return on_device(*args)

    return jax.shard_map(
        body, mesh=mesh, in_specs=in_specs, out_specs=out_specs, check_vma=False
    )
```

```python
import functools

import jax
import jax.numpy as jnp
from jax import lax
from jax.experimental import pallas as pl
from jax.experimental.pallas import tpu as pltpu
from jax.sharding import PartitionSpec as P

GROUPS = 4


highest = lax.Precision.HIGHEST


def split_columns(values, order, rank_width, group_mask):
    count = values.shape[0]
    experts_here = order.shape[0]
    half = experts_here // 2
    taken = jnp.take(values.reshape(count, experts_here, rank_width), order, axis=1)
    image_part = taken[:, :half].reshape(count, half * rank_width)
    text_part = taken[:, half:].reshape(count, half * rank_width)
    return (image_part, group_mask[:, None, None] * text_part)


def join_columns(image_sum, text_slots, rank_of, group_mask, rank_width, replicas, group_size):
    count = image_sum.shape[0]
    half = image_sum.shape[1] // rank_width
    image_mean = (image_sum / replicas).reshape(count, half, rank_width)
    text_mean = (jnp.sum(group_mask[:, None, None] * text_slots, axis=0) / group_size).reshape(
        count, half, rank_width
    )
    joined = jnp.concatenate([image_mean, text_mean], axis=1)
    return jnp.take(joined, rank_of, axis=1).reshape(count, 2 * half * rank_width)


def on_device(x_act, d_out, error, q_init, modality, membership):
    tok_x = x_act[0]
    grads_out = d_out[0]
    residual = error[0]
    experts_here, row_count, hidden = residual.shape
    rank_width = q_init.shape[1] // experts_here
    replicas = membership.shape[0]
    groups = GROUPS
    group_size = replicas // groups
    my_group = membership[lax.axis_index("dp")]
    group_mask = (jnp.arange(groups) == my_group).astype(jnp.float32)
    order = jnp.argsort(modality, stable=True)
    rank_of = jnp.argsort(order, stable=True)
    gradient = jnp.einsum("ktd,kth->kdh", tok_x, grads_out, preferred_element_type=jnp.float32)
    merged = (gradient + residual.astype(jnp.float32)).astype(jnp.bfloat16)
    q_blocks = q_init.reshape(hidden, experts_here, rank_width)
    left_part = jnp.einsum("kdh,hkr->dkr", merged, q_blocks, preferred_element_type=jnp.float32)
    left_part = left_part.reshape(row_count, experts_here * rank_width)
    image_part, text_part = split_columns(left_part, order, rank_width, group_mask)
    image_sum, text_slots = lax.psum((image_part, text_part), "dp")
    left_mean = join_columns(
        image_sum, text_slots, rank_of, group_mask, rank_width, replicas, group_size
    )
    blocks = left_mean.reshape(row_count, experts_here, rank_width)
    local_gram = jnp.einsum("dkr,dks->krs", blocks, blocks, precision=highest)
    gram_block = lax.psum(local_gram, "expert")
    identity = jnp.eye(rank_width, dtype=jnp.float32)
    shift_term = 0.001 * jnp.trace(gram_block, axis1=1, axis2=2) / rank_width
    factor_low = jnp.linalg.cholesky(gram_block + shift_term[:, None, None] * identity)
    inverse = jax.scipy.linalg.solve_triangular(
        factor_low, jnp.broadcast_to(identity, factor_low.shape), lower=True
    )
    p_hat = jnp.einsum("dkr,ksr->dks", blocks, inverse, precision=highest).astype(jnp.bfloat16)
    part_q = jnp.einsum("kdh,dkr->hkr", merged, p_hat, preferred_element_type=jnp.float32)
    q_local = part_q.reshape(hidden, experts_here * rank_width)
    image_part, text_part = split_columns(q_local, order, rank_width, group_mask)
    image_sum, text_slots = lax.psum((image_part, text_part), ("dp", "expert"))
    q_mean = join_columns(
        image_sum, text_slots, rank_of, group_mask, rank_width, replicas, group_size
    )
    q_sum = q_mean.astype(jnp.bfloat16)
    approx = jnp.einsum(
        "dkr,hkr->kdh",
        p_hat,
        q_sum.reshape(hidden, experts_here, rank_width),
        preferred_element_type=jnp.float32,
    )
    error_new = (merged.astype(jnp.float32) - approx).astype(jnp.bfloat16)
    return (q_sum[None], error_new[None])


MESH = pl.DeviceIdType.MESH
F32 = jnp.float32
BF16 = jnp.bfloat16


def compress_kernel(
    n_dp, n_ex, group_size,
    x_hbm, d_hbm, err_hbm, q_hbm, modality_hbm, membership_hbm,
    merged_hbm, pt_ref, qt_out,
    q_ref, modality, membership, xs, ds, merged, lsend, lrecv, msend, lmean, gsend, grecv,
    qpart, qr1, qs2, qr2, q3, qr3, q4, qf,
    in_sem, x_sem, d_sem, e_sem, m_sem, ls_sem, lr_sem, ms_sem, mr_sem, gs_sem, gr_sem,
    s1_sem, r1_sem, s2_sem, r2_sem, s3_sem, r3_sem, s4_sem, r4_sem,
    s5_sem, r5_sem,
):
    dp = lax.axis_index("dp")
    ex = lax.axis_index("expert")
    core, row = ex % 2, ex // 2
    ex_core = row * 2 + (1 - core)
    ex_row = (1 - row) * 2 + core
    ex_far = (1 - row) * 2 + (1 - core)
    experts, tokens, rows = xs.shape
    hidden = ds.shape[2]
    width = q_ref.shape[1]
    rank = width // experts
    step_rows = rows // n_dp
    slab = hidden // n_ex
    part = width // n_dp

    def remote(src, dst, send, recv, dp_to, ex_to):
        return pltpu.make_async_remote_copy(
            src_ref=src, dst_ref=dst, send_sem=send, recv_sem=recv,
            device_id=(dp_to, ex_to), device_id_type=MESH,
        )

    def rows_of(c, size):
        return pl.ds(pl.multiple_of(c * size, size), size)

    twos = n_dp // 2
    two_rows = 2 * step_rows

    def two_of(s):
        return (dp // 2 + 1 + s) % twos

    def err_copy(s):
        at = rows_of(two_of(s), two_rows)
        return pltpu.make_async_copy(err_hbm.at[:, at, :], merged.at[:, at, :], e_sem.at[s])

    def merged_copy(s):
        at = rows_of(two_of(s), two_rows)
        return pltpu.make_async_copy(merged.at[:, at, :], merged_hbm.at[:, at, :], m_sem.at[s])

    x_copies = [pltpu.make_async_copy(x_hbm.at[k], xs.at[k], x_sem.at[k]) for k in range(experts)]
    d_copies = [pltpu.make_async_copy(d_hbm.at[k], ds.at[k], d_sem.at[k]) for k in range(experts)]
    for k in range(experts):
        x_copies[k].start()
        d_copies[k].start()
    small = [
        pltpu.make_async_copy(src, dst, in_sem.at[n])
        for n, (src, dst) in enumerate(
            ((q_hbm, q_ref), (modality_hbm, modality), (membership_hbm, membership))
        )
    ]
    for copy in small:
        copy.start()
    for s in range(twos):
        err_copy(s).start()

    barrier = pltpu.get_barrier_semaphore()
    for s in range(1, n_dp):
        pl.semaphore_signal(barrier, inc=1, device_id=((dp + s) % n_dp, ex), device_id_type=MESH)
    for other in (ex_core, ex_row, ex_far):
        pl.semaphore_signal(barrier, inc=1, device_id=(dp, other), device_id_type=MESH)
    pl.semaphore_wait(barrier, n_dp - 1 + 3)

    for k in range(experts):
        x_copies[k].wait()
        d_copies[k].wait()
    for copy in small:
        copy.wait()

    lane = lax.broadcasted_iota(jnp.int32, (1, width), 1)

    def left_copy(c, src):
        return remote(lsend.at[c], lrecv.at[src], ls_sem.at[c], lr_sem.at[src], c, ex)

    def left_step(s, carry):
        two = two_of(s)
        at = rows_of(two, two_rows)
        err_copy(s).wait()
        total = jnp.zeros((two_rows, width), F32)
        for k in range(experts):
            xk = xs[k, :, at]
            for n in range(hidden // 256):
                cols = slice(n * 256, (n + 1) * 256)
                grad = lax.dot_general(
                    xk, ds[k, :, cols], (((0,), (0,)), ((), ())), preferred_element_type=F32
                )
                merged[k, at, cols] = (grad + merged[k, at, cols].astype(F32)).astype(BF16)
            mine = jnp.dot(merged[k, at, :], q_ref[...], preferred_element_type=F32)
            total += jnp.where(lane // rank == k, mine, 0.0)
        merged_copy(s).start()
        for h in range(2):
            c = 2 * two + h
            block = total[h * step_rows : (h + 1) * step_rows, :].astype(BF16)

            @pl.when(c != dp)
            def _():
                lsend[c] = block
                left_copy(c, dp).start()

            @pl.when(c == dp)
            def _():
                lrecv[dp] = block

        return carry

    lax.fori_loop(0, twos, left_step, 0)

    def wait_left(s, carry):
        left_copy((dp + s) % n_dp, (dp + n_dp - s) % n_dp).wait_recv()
        return carry

    lax.fori_loop(1, n_dp, wait_left, 0)

    image = jnp.zeros((1, width), F32)
    for k in range(experts):
        flag = jnp.where(modality[k] == 0, 1.0, 0.0)
        image = jnp.where(lane // rank == k, flag, image)

    def mean_copy(i, src):
        return remote(msend.at[i], lmean.at[src], ms_sem.at[i], mr_sem.at[src], i, ex)

    def mean_step(s, carry):
        i = (dp + 1 + s) % n_dp
        acc = jnp.zeros((step_rows, width), F32)
        for j in range(n_dp):
            same = jnp.where(membership[i] == membership[j], 1.0 / group_size, 0.0)
            weight = jnp.where(image > 0.5, 1.0 / n_dp, same)
            acc += weight * lrecv[j].astype(F32)

        @pl.when(s < n_dp - 1)
        def _():
            msend[i] = acc.astype(BF16)
            mean_copy(i, dp).start()

        @pl.when(s == n_dp - 1)
        def _():
            lmean[dp] = acc.astype(BF16)

        return carry

    lax.fori_loop(0, n_dp, mean_step, 0)

    def gram_of(j):
        block = lmean[j]
        return lax.dot_general(block, block, (((0,), (0,)), ((), ())), preferred_element_type=F32)

    def gram_step(s, acc):
        j = (dp + n_dp - s) % n_dp
        mean_copy((dp + s) % n_dp, j).wait_recv()
        return acc + gram_of(j)

    gram = lax.fori_loop(1, n_dp, gram_step, gram_of(dp))
    pairs = experts // 2
    pair_lane = lax.broadcasted_iota(jnp.int32, (rank, 2 * rank), 1)
    pair_row = lax.broadcasted_iota(jnp.int32, (rank, 2 * rank), 0)
    low = pair_lane < rank
    for p in range(pairs):
        b = 2 * p * rank
        gsend[p] = jnp.where(
            low, gram[b : b + rank, b : b + 2 * rank], gram[b + rank : b + 2 * rank, b : b + 2 * rank]
        )
    grecv[ex] = gsend[...]
    others = (ex_core, ex_row, ex_far)
    gram_sends = [
        remote(gsend, grecv.at[ex], gs_sem.at[n], gr_sem.at[n], dp, other)
        for n, other in enumerate(others)
    ]
    for copy in gram_sends:
        copy.start()
    for n, other in enumerate(others):
        remote(gsend, grecv.at[other], gs_sem.at[n], gr_sem.at[n], dp, other).wait_recv()
    full = grecv[0]
    for e in range(1, n_ex):
        full = full + grecv[e]

    spots = (pair_lane == pair_row, pair_lane == pair_row + rank)
    work = []
    for odd in range(2):
        diag, unit = spots[odd], spots[1 - odd]
        trace = jnp.sum(jnp.where(diag, full, 0.0), axis=(1, 2), keepdims=True)
        a = full + jnp.where(diag, 0.001 * trace / rank, 0.0)
        here = low if odd == 0 else jnp.logical_not(low)
        work.append(jnp.where(here, a, jnp.where(unit, 1.0, 0.0)))
    done = [[], []]
    panel = 4
    for j in range(0, rank, panel):
        left_rows = rank - j // 8 * 8
        at_row = lax.broadcasted_iota(jnp.int32, (1, left_rows, 1), 1)
        for odd in range(2):
            w = work[odd]
            columns = [
                jnp.broadcast_to(w[:, :, at : at + 1], w.shape)
                for at in range(j + odd * rank, j + odd * rank + panel)
            ]
            for m in range(panel):
                r = j % 8 + m
                inverse_pivot = 1.0 / columns[m][:, r : r + 1, :]
                factor = jnp.where(at_row > r, columns[m], 0.0) * inverse_pivot
                for n in range(m + 1, panel):
                    columns[n] = columns[n] - factor * columns[n][:, r : r + 1, :]
                w = w - factor * w[:, r : r + 1, :]
            work[odd] = w
        if (j + panel) % 8 == 0:
            for odd in range(2):
                done[odd].append(work[odd][:, :8, :])
                work[odd] = work[odd][:, 8:, :]
    blocks = []
    for p in range(pairs):
        for odd in range(2):
            w = jnp.concatenate([chunk[p] for chunk in done[odd]], axis=0)
            pivots = jnp.sum(jnp.where(spots[odd], w, 0.0), axis=1, keepdims=True)
            keep = jnp.logical_not(low) if odd == 0 else low
            inverse = jnp.where(keep, w, 0.0) / jnp.sqrt(pivots)
            inverse = pltpu.roll(inverse, rank, 1)
            zero = jnp.zeros((rank, 2 * rank), F32)
            blocks.append(
                jnp.concatenate([inverse if q == p else zero for q in range(pairs)], axis=1)
            )
    inv = jnp.concatenate(blocks, axis=0)
    inv_high = inv.astype(BF16)
    inv_low = (inv - inv_high.astype(F32)).astype(BF16)
    for j in range(n_dp):
        block = lmean[j]
        dims = (((1,), (1,)), ((), ()))
        p_t = lax.dot_general(inv_high, block, dims, preferred_element_type=F32)
        p_t += lax.dot_general(inv_low, block, dims, preferred_element_type=F32)
        pt_ref[:, j * step_rows : (j + 1) * step_rows] = p_t.astype(BF16)

    def k_rows(k):
        return pl.ds(k * rank, rank)

    def core_copy(k, n):
        slab_at = (ex_core, ex_far)[n]
        return remote(
            qpart.at[slab_at, k_rows(k), :], qr1.at[n, k_rows(k), :],
            s1_sem.at[n, k], r1_sem.at[n, k], dp, ex_core,
        )

    def row_copy(k):
        return remote(
            qs2.at[k_rows(k), :], qr2.at[k_rows(k), :], s2_sem.at[k], r2_sem.at[k], dp, ex_row
        )

    def part_copy(c, src):
        return remote(
            q3.at[rows_of(c, part), :], qr3.at[src], s3_sem.at[c], r3_sem.at[src], c, ex
        )

    per = rank // part

    def stage_one(k):
        p_k = pt_ref[k * rank : (k + 1) * rank, :]
        for e in range(n_ex):
            out = jnp.dot(
                p_k, merged[k, :, e * slab : (e + 1) * slab], preferred_element_type=F32
            )
            qpart[e, k * rank : (k + 1) * rank, :] = out.astype(BF16)
        core_copy(k, 1).start()
        core_copy(k, 0).start()

    def stage_two(k):
        core_copy(k, 1).wait_recv()
        at = slice(k * rank, (k + 1) * rank)
        qs2[at, :] = (qpart[ex_row, at, :].astype(F32) + qr1[1, at, :].astype(F32)).astype(BF16)
        row_copy(k).start()

    def stage_three(k):
        core_copy(k, 0).wait_recv()
        row_copy(k).wait_recv()
        at = slice(k * rank, (k + 1) * rank)
        q3[at, :] = (
            qpart[ex, at, :].astype(F32) + qr1[0, at, :].astype(F32) + qr2[at, :].astype(F32)
        ).astype(BF16)
        for c in range(k * per, (k + 1) * per):

            @pl.when(dp != c)
            def _():
                part_copy(c, dp).start()

            @pl.when(dp == c)
            def _():
                qr3[c] = q3[c * part : (c + 1) * part, :]

    for k in range(experts + 2):
        if k < experts:
            stage_one(k)
        if 1 <= k <= experts:
            stage_two(k - 1)
        if k >= 2:
            stage_three(k - 2)

    def wait_part(s, carry):
        part_copy((dp + s) % n_dp, (dp + n_dp - s) % n_dp).wait_recv()
        return carry

    lax.fori_loop(1, n_dp, wait_part, 0)
    my_image = modality[dp // per] == 0

    def back_copy(i, src):
        return remote(
            q4.at[i], qf.at[ex, rows_of(src, part), :], s4_sem.at[i], r4_sem.at[src], i, ex
        )

    def back_step(s, carry):
        i = (dp + 1 + s) % n_dp
        acc = jnp.zeros((part, slab), F32)
        for j in range(n_dp):
            same = jnp.where(membership[i] == membership[j], 1.0 / group_size, 0.0)
            acc += jnp.where(my_image, 1.0 / n_dp, same) * qr3[j].astype(F32)

        @pl.when(s < n_dp - 1)
        def _():
            q4[i] = acc.astype(BF16)
            back_copy(i, dp).start()

        @pl.when(s == n_dp - 1)
        def _():
            qf[ex, rows_of(dp, part), :] = acc.astype(BF16)

        return carry

    lax.fori_loop(0, n_dp, back_step, 0)

    def spread(c, n):
        held, to = ((ex, ex_core), (ex, ex_row), (ex_row, ex_core))[n]
        at = rows_of(c, part)
        return remote(
            qf.at[held, at, :], qf.at[held, at, :], s5_sem.at[n, c], r5_sem.at[n, c], dp, to
        )

    def spread_step(s, carry):
        c = (dp + n_dp - s) % n_dp

        @pl.when(s > 0)
        def _():
            back_copy((dp + s) % n_dp, c).wait_recv()

        spread(c, 1).start()
        spread(c, 0).start()
        return carry

    lax.fori_loop(0, n_dp, spread_step, 0)

    def forward_step(s, carry):
        c = (dp + n_dp - s) % n_dp
        spread(c, 1).wait_recv()
        spread(c, 2).start()
        return carry

    lax.fori_loop(0, n_dp, forward_step, 0)

    def last_step(s, carry):
        c = (dp + n_dp - s) % n_dp
        spread(c, 0).wait_recv()
        spread(c, 2).wait_recv()
        return carry

    lax.fori_loop(0, n_dp, last_step, 0)
    for e in range(n_ex):
        qt_out[:, e * slab : (e + 1) * slab] = qf[e]

    def drain(s, carry):
        i = (dp + s) % n_dp
        left_copy(i, dp).wait_send()
        mean_copy(i, dp).wait_send()
        part_copy(i, dp).wait_send()
        back_copy(i, dp).wait_send()
        return carry

    lax.fori_loop(1, n_dp, drain, 0)

    def drain_all(c, carry):
        for n in range(3):
            spread(c, n).wait_send()
        return carry

    lax.fori_loop(0, n_dp, drain_all, 0)
    for s in range(twos):
        merged_copy(s).wait()
    for k in range(experts):
        core_copy(k, 0).wait_send()
        core_copy(k, 1).wait_send()
        row_copy(k).wait_send()
    for copy in gram_sends:
        copy.wait_send()


def residual_kernel(
    pt_ref, qt_ref, merged, err_hbm, q_hbm, stage, q_stage, m_sem, e_sem, q_sem
):
    experts, rows, hidden = merged.shape
    rank = pt_ref.shape[0] // experts
    pieces, size = stage.shape[:2]
    per = rows // size

    def place(ref, t):
        return ref.at[t // per, pl.ds(pl.multiple_of((t % per) * size, size), size), :]

    def load(t):
        return pltpu.make_async_copy(place(merged, t), stage.at[t], m_sem.at[t])

    def copy(t):
        return pltpu.make_async_copy(stage.at[t], place(err_hbm, t), e_sem.at[t])

    for t in range(pieces):
        load(t).start()

    def step(t, carry):
        at = pl.ds(pl.multiple_of((t % per) * size, size), size)
        of = pl.ds(pl.multiple_of((t // per) * rank, rank), rank)
        p_rows = pt_ref[of, at]
        load(t).wait()
        for n in range(hidden // 256):
            cols = slice(n * 256, (n + 1) * 256)
            approx = lax.dot_general(
                p_rows, qt_ref[of, cols], (((0,), (0,)), ((), ())), preferred_element_type=F32
            )
            stage[t, :, cols] = (stage[t, :, cols].astype(F32) - approx).astype(BF16)
        copy(t).start()
        return carry

    lax.fori_loop(0, pieces, step, 0)
    q_stage[...] = qt_ref[...].T
    q_copy = pltpu.make_async_copy(q_stage, q_hbm, q_sem)
    q_copy.start()

    def wait(t, carry):
        copy(t).wait()
        return carry

    lax.fori_loop(0, pieces, wait, 0)
    q_copy.wait()


def tiled_form(n_dp, n_ex, x_act, d_out, error, q_init, modality, membership):
    experts, tokens, rows = x_act.shape[1:]
    hidden = d_out.shape[3]
    width = q_init.shape[1]
    rank = width // experts
    slab, part, step_rows = hidden // n_ex, width // n_dp, rows // n_dp
    group_size = membership.shape[0] // GROUPS
    any_spec = pl.BlockSpec(memory_space=pl.ANY)
    vmem = pl.BlockSpec(memory_space=pltpu.VMEM)
    dma = pltpu.SemaphoreType.DMA
    merged, p_t, q_t = pl.pallas_call(
        functools.partial(compress_kernel, n_dp, n_ex, group_size),
        out_shape=(
            jax.ShapeDtypeStruct((experts, rows, hidden), BF16),
            jax.ShapeDtypeStruct((width, rows), BF16),
            jax.ShapeDtypeStruct((width, hidden), BF16),
        ),
        in_specs=[any_spec] * 6,
        out_specs=(any_spec, vmem, vmem),
        scratch_shapes=[
            pltpu.VMEM((hidden, width), BF16),
            pltpu.SMEM(modality.shape, jnp.int32),
            pltpu.SMEM(membership.shape, jnp.int32),
            pltpu.VMEM((experts, tokens, rows), BF16),
            pltpu.VMEM((experts, tokens, hidden), BF16),
            pltpu.VMEM((experts, rows, hidden), BF16),
            pltpu.VMEM((n_dp, step_rows, width), BF16),
            pltpu.VMEM((n_dp, step_rows, width), BF16),
            pltpu.VMEM((n_dp, step_rows, width), BF16),
            pltpu.VMEM((n_dp, step_rows, width), BF16),
            pltpu.VMEM((experts // 2, rank, 2 * rank), F32),
            pltpu.VMEM((n_ex, experts // 2, rank, 2 * rank), F32),
            pltpu.VMEM((n_ex, width, slab), BF16),
            pltpu.VMEM((2, width, slab), BF16),
            pltpu.VMEM((width, slab), BF16),
            pltpu.VMEM((width, slab), BF16),
            pltpu.VMEM((width, slab), BF16),
            pltpu.VMEM((n_dp, part, slab), BF16),
            pltpu.VMEM((n_dp, part, slab), BF16),
            pltpu.VMEM((n_ex, width, slab), BF16),
            dma((3,)), dma((experts,)), dma((experts,)), dma((n_dp // 2,)), dma((n_dp // 2,)),
            dma((n_dp,)), dma((n_dp,)), dma((n_dp,)), dma((n_dp,)),
            dma((3,)), dma((3,)),
            dma((2, experts)), dma((2, experts)), dma((experts,)), dma((experts,)),
            dma((n_dp,)), dma((n_dp,)), dma((n_dp,)), dma((n_dp,)),
            dma((3, n_dp)), dma((3, n_dp)),
        ],
        compiler_params=pltpu.CompilerParams(
            collective_id=0, has_side_effects=True, vmem_limit_bytes=56 * 2**20
        ),
        cost_estimate=pl.CostEstimate(
            flops=12 * experts * rows * hidden * tokens // 4,
            bytes_accessed=4 * experts * rows * hidden,
            transcendentals=0,
        ),
        name="compress",
    )(x_act[0], d_out[0], error[0], q_init, modality, membership)
    block = rows // 4
    error_new, q_sum = pl.pallas_call(
        residual_kernel,
        out_shape=(
            jax.ShapeDtypeStruct((experts, rows, hidden), BF16),
            jax.ShapeDtypeStruct((hidden, width), BF16),
        ),
        in_specs=[vmem, vmem, any_spec],
        out_specs=(any_spec, any_spec),
        scratch_shapes=[
            pltpu.VMEM((experts * rows // block, block, hidden), BF16),
            pltpu.VMEM((hidden, width), BF16),
            dma((experts * rows // block,)),
            dma((experts * rows // block,)),
            dma,
        ],
        compiler_params=pltpu.CompilerParams(vmem_limit_bytes=56 * 2**20),
        name="residual",
    )(p_t, q_t, merged)
    return (q_sum[None], error_new[None])


def tiles(n_dp, n_ex, x_act, d_out, error, q_init, modality, membership):
    experts, _, rows = x_act.shape[1:]
    hidden, width = q_init.shape
    rank = width // experts
    return (
        n_ex == 4
        and experts % 2 == 0
        and 2 * rank == 128
        and rank % (width // n_dp) == 0
        and (width // n_dp) % 16 == 0
        and (rows // n_dp) % 128 == 0
        and (hidden // n_ex) % 128 == 0
        and hidden % 256 == 0
    )


def solution(mesh):
    in_specs = (
        P("dp", None, None, "expert"),
        P("dp", None, None, None),
        P("dp", None, "expert", None),
        P(),
        P(),
        P(),
    )
    out_specs = (P("dp", None, None), P("dp", None, "expert", None))
    n_dp, n_ex = mesh.shape["dp"], mesh.shape["expert"]

    def body(*args):
        if tiles(n_dp, n_ex, *args):
            return tiled_form(n_dp, n_ex, *args)
        return on_device(*args)

    return jax.shard_map(
        body, mesh=mesh, in_specs=in_specs, out_specs=out_specs, check_vma=False
    )
```
